128 devices in a mesh: gx: 4 (over x), gy: 32 (over y, z, core).
Axes of the slice: x: 4, y: 4, z: 4, core: 2. Of those that a mesh axis runs over, the one named last changes fastest.
Arguments:
- multipole: bfloat16 [32768, 256], P(('gx', 'gy')), may hold values from -6 to 6
- coarse_multipole: bfloat16 [4096, 256], P(('gx', 'gy')), may hold values from -6 to 6
- operators: bfloat16 [48, 256, 256], replicated, may hold values from -0.0390625 to 0.0390625
- source_list: int32 [32768, 189], P(('gx', 'gy')), may hold values from 0 to 32767, as said below
- op_list: int32 [32768, 189], P(('gx', 'gy')), may hold values from 0 to 47
- list_count: int32 [32768], P(('gx', 'gy')), may hold values from 1 to 189, as said below
- coarse_src: int32 [32768, 27], P(('gx', 'gy')), may hold values from 0 to 4095
- coarse_op: int32 [32768, 27], P(('gx', 'gy')), may hold values from 0 to 47
Outputs:
- local_expansion: float32 [32768, 256], P(('gx', 'gy'))
The draws below stay inside these ranges and needn't reach their ends.
Inputs may be any that keep to these rules, and one draw needn't show every extreme that they name: source_list[t, j] is a block of owner(t) - 1, owner(t) or owner(t) + 1 (owner(b) = b // 256). `list_count`: the first block of every device uses all 189 slots.
All inputs are finite; a program needn't handle non-finite values.
Results may differ from the reference program's by a relative error of at most 0.0055.
Values may be sent and summed in bfloat16 or wider, within the bound.
A program may use at most 128 MiB of HBM per device.

```python
import jax
import jax.numpy as jnp
from jax import lax

P_SIZE = 256
LIST = 189
CLIST = 27
NOPS = 48
BLK_DEV = 256
BLOCKS = 32768
CBLK = 4096


def draw_source_list(key, part):
    key = jax.random.fold_in(key, 1)
    owner_dev = jnp.arange(BLOCKS, dtype=jnp.int32) // BLK_DEV
    offset = jax.random.randint(key, (BLOCKS, LIST), -BLK_DEV, 2 * BLK_DEV, dtype=jnp.int32)
    return jnp.clip(owner_dev[:, None] * BLK_DEV + offset, 0, BLOCKS - 1).astype(jnp.int32)


def draw_list_count(key, part):
    key = jax.random.fold_in(key, 2)
    heavy_key = jax.random.fold_in(key, 5)
    count_key = jax.random.fold_in(key, 7)
    owner_dev = jnp.arange(BLOCKS, dtype=jnp.int32) // BLK_DEV
    heavy = jax.random.randint(heavy_key, (BLOCKS // BLK_DEV,), 0, 4, dtype=jnp.int32) == 0
    heavy_block = heavy[owner_dev]
    lowest = jnp.where(heavy_block, LIST // 2 + 1, 1).astype(jnp.int32)
    highest = jnp.where(heavy_block, LIST + 1, LIST // 4 + 2).astype(jnp.int32)
    raw = jax.random.randint(count_key, (BLOCKS,), 0, 1 << 20, dtype=jnp.int32)
    counts = lowest + raw % (highest - lowest)
    first = jnp.arange(BLOCKS, dtype=jnp.int32) % BLK_DEV == 0
    return jnp.where(first, LIST, counts).astype(jnp.int32)


def with_ends(drawn, stream_key, low, top_value):
    longest = drawn.shape.index(max(drawn.shape))
    spots = []
    for shift in (0, 1):
        where = [jax.random.randint(jax.random.fold_in(stream_key, axis), (), 0, length) for axis, length in enumerate(drawn.shape)]
        where[longest] = (where[longest] + shift) % drawn.shape[longest]
        spots.append(tuple(where))
    return drawn.at[spots[0]].set(low).at[spots[1]].set(top_value)


def level_of(stream_key, extent, split, least, largest):
    gain, own = 1.0, jax.random.fold_in(stream_key, 6)
    for axis_at, parts in split:
        draws = jnp.exp(jax.random.uniform(jax.random.fold_in(own, axis_at), (parts,), jnp.float32, least / len(split), largest / len(split)))
        gain = gain * jnp.repeat(draws, extent[axis_at] // parts).reshape([-1 if axis == axis_at else 1 for axis in range(len(extent))])
    return gain


def noise(rng, dims, scale, reach, shards=(), kind=jnp.bfloat16):
    values = scale * jax.random.normal(rng, dims, jnp.float32)
    if shards:
        values = values * level_of(rng, dims, shards, -0.22, 0.18)
    return jnp.clip(values, -reach, reach).astype(kind)


def setup_inputs(seed: int = 0) -> dict:
    key_of = jax.random.split(jax.random.key(seed), 9)
    multipole = noise(key_of[0], (BLOCKS, P_SIZE), 1.0, 6.0, ((0, 128),))
    coarse_multipole = noise(key_of[1], (CBLK, P_SIZE), 1.0, 6.0, ((0, 128),))
    operators = noise(key_of[2], (NOPS, P_SIZE, P_SIZE), (P_SIZE * LIST // 2) ** -0.5, 0.0390625)
    source_list = draw_source_list(jax.random.fold_in(key_of[8], 71), 0)
    op_list = with_ends(jax.random.randint(key_of[4], (BLOCKS, LIST), 0, NOPS), jax.random.fold_in(key_of[4], 1), 0, NOPS - 1).astype(jnp.int32)
    list_count = draw_list_count(jax.random.fold_in(key_of[8], 71), 0)
    coarse_src = with_ends(jax.random.randint(key_of[6], (BLOCKS, CLIST), 0, CBLK), jax.random.fold_in(key_of[6], 1), 0, CBLK - 1).astype(jnp.int32)
    coarse_op = with_ends(jax.random.randint(key_of[7], (BLOCKS, CLIST), 0, NOPS), jax.random.fold_in(key_of[7], 1), 0, NOPS - 1).astype(jnp.int32)
    return {"multipole": multipole, "coarse_multipole": coarse_multipole, "operators": operators, "source_list": source_list, "op_list": op_list, "list_count": list_count, "coarse_src": coarse_src, "coarse_op": coarse_op}


def device_rows(d, multipole, coarse_multipole, operators, source_list, op_list, list_count, coarse_src, coarse_op):
    width = 3 * BLK_DEV
    zeros_pad = jnp.zeros((BLK_DEV, P_SIZE), jnp.bfloat16)
    padded = jnp.concatenate([zeros_pad, multipole, zeros_pad], axis=0)
    window = lax.dynamic_slice(padded, (d * BLK_DEV, jnp.int32(0)), (width, P_SIZE)).astype(jnp.float32)
    start = (d * BLK_DEV).astype(jnp.int32)
    rows = lax.dynamic_slice_in_dim(source_list, start, BLK_DEV, 0)
    ops = lax.dynamic_slice_in_dim(op_list, start, BLK_DEV, 0)
    counts = lax.dynamic_slice_in_dim(list_count, start, BLK_DEV, 0)
    located = rows - (d - 1) * BLK_DEV
    valid = jnp.arange(LIST, dtype=jnp.int32)[None, :] < counts[:, None]
    op_hot = ((ops[:, :, None] == jnp.arange(NOPS, dtype=jnp.int32)) & valid[:, :, None]).astype(jnp.float32)
    src_hot = (located[:, :, None] == jnp.arange(width, dtype=jnp.int32)).astype(jnp.float32)
    tally = jnp.einsum("tjr,tjc->trc", op_hot, src_hot)
    tally = tally.reshape(BLK_DEV, NOPS, 3, BLK_DEV)
    group = jnp.einsum("trsc,scp->tsrp", tally, window.reshape(3, BLK_DEV, P_SIZE)).astype(jnp.bfloat16)
    opf = operators.astype(jnp.float32)
    near = jnp.einsum("tsrp,rqp->tq", group.astype(jnp.float32), opf)
    crow = lax.dynamic_slice_in_dim(coarse_src, start, BLK_DEV, 0)
    cops = lax.dynamic_slice_in_dim(coarse_op, start, BLK_DEV, 0)
    picked = coarse_multipole[crow].astype(jnp.float32)
    cop_hot = (cops[:, :, None] == jnp.arange(NOPS, dtype=jnp.int32)).astype(jnp.float32)
    coarse_group = jnp.einsum("tjr,tjp->trp", cop_hot, picked).astype(jnp.bfloat16)
    far = jnp.einsum("trp,rqp->tq", coarse_group.astype(jnp.float32), opf)
    return near + far


def reference(multipole, coarse_multipole, operators, source_list, op_list, list_count, coarse_src, coarse_op):
    devices_total = BLOCKS // BLK_DEV
    result = lax.map(lambda d: device_rows(d, multipole, coarse_multipole, operators, source_list, op_list, list_count, coarse_src, coarse_op), jnp.arange(devices_total, dtype=jnp.int32))
    return result.reshape(BLOCKS, P_SIZE)
```

```python
import functools

import jax
import jax.numpy as jnp
from jax import lax
from jax.experimental import pallas as pl
from jax.experimental.pallas import tpu as pltpu
from jax.sharding import PartitionSpec as P

TARGETS = 256
SLOTS = 189
COARSE_SLOTS = 27
NOPS = 48
COEFFS = 256
STEP = 16
F8 = jnp.float8_e4m3fn
BF16 = jnp.bfloat16
F32 = jnp.float32
LAST = (((1,), (1,)), ((), ()))
MESH = pl.DeviceIdType.MESH

ORDERS = ((2, 1, 0), (0, 2, 1), (1, 0, 2), (2, 1, 0))


def one_hot_rows(row, blocks):
    number = lax.broadcasted_iota(jnp.int32, row.shape, 0).astype(F32)
    one, zero = BF16(1), BF16(0)
    return jnp.concatenate(
        [jnp.where(row == (number + 16.0 * k).astype(BF16), one, zero) for k in range(blocks)], axis=0
    )


def transpose8(v):
    row = lax.broadcasted_iota(jnp.int32, v[0].shape, 0)
    cur = [v[0]] + [pltpu.roll(v[k], k, 0) for k in range(1, 8)]
    for bit in (1, 2, 4):
        odd = (row & bit) != 0
        cur = [jnp.where(odd, cur[(k + bit) % 8], cur[k]) for k in range(8)]
    return [cur[0]] + [pltpu.roll(cur[8 - r], 8 - r, 0) for r in range(1, 8)]


def kernel(
    multipole, coarse, operators, source_t, op_t, count, coarse_src_t, coarse_op_t,
    out,
    window, received, table, ops, src_v, op_v, count_v, cop_v, csrc, slot_q, slot_c, slot_cop, tmp, tally, picked0, picked1, group,
    local_sem, send_sem, recv_sem, sib_send, sib_recv, halo_send, halo_recv,
):
    x = lax.axis_index("gx")
    gy = lax.axis_index("gy")
    y, z, core = lax.div(gy, 8), lax.rem(lax.div(gy, 2), 4), lax.rem(gy, 2)
    coords = (x, y, z)
    me = x * 32 + gy

    def device(cx, cy, cz, cc):
        return (cx, (cy * 4 + cz) * 2 + cc)

    def linear(d):
        return (lax.div(d, 32), lax.rem(d, 32))

    def local(src, dst, k):
        return pltpu.make_async_copy(src, dst, local_sem.at[k])

    rows16 = lambda f, pos, n: received.at[f, pl.ds(pl.multiple_of(pos * 16, 16), n * 16), :]
    flow = [core * 2 + h for h in range(2)]
    at = []
    for h in range(2):
        at.append([coords[ORDERS[h][s]] * (1 - core) + coords[ORDERS[2 + h][s]] * core for s in range(3)])

    def region(h, stage, last=None):
        a, b, c = at[h]
        c = c if last is None else last
        if stage == 0:
            return rows16(flow[h], c * 16 + b * 4 + a, 1)
        if stage == 1:
            return rows16(flow[h], c * 16 + b * 4, 4)
        return rows16(flow[h], c * 16, 16)

    own = [local(coarse.at[pl.ds(h * 16, 16), :], region(h, 0), h) for h in range(2)]
    mid = local(multipole, window.at[pl.ds(256, 256), :], 2)
    lists = [
        local(source_t, src_v, 3), local(op_t, op_v, 4), local(count, count_v, 5), local(coarse_op_t, cop_v, 6),
        local(coarse_src_t, csrc, 7),
    ]
    weights = local(operators, ops, 8)
    for c in own + [mid] + lists + [weights]:
        c.start()

    barrier = pltpu.get_barrier_semaphore()
    after, before = linear(lax.rem(me + 1, 128)), linear(lax.rem(me + 127, 128))
    partners = [device(x, y, z, 1 - core), after, before]
    for axis in range(3):
        for k in range(1, 4):
            other = list(coords)
            other[axis] = lax.rem(coords[axis] + k, 4)
            partners.append(device(*other, core))
    for p in partners:
        pl.semaphore_signal(barrier, inc=1, device_id=p, device_id_type=MESH)

    def hop(h, stage, k):
        other = list(coords)
        for c, weight in ((0, 1 - core), (1, core)):
            axis = ORDERS[2 * c + h][stage]
            other[axis] = other[axis] + weight * (lax.rem(coords[axis] + k, 4) - coords[axis])
        part = region(h, stage)
        return pltpu.make_async_remote_copy(
            src_ref=part, dst_ref=part, send_sem=send_sem.at[h, stage, k - 1], recv_sem=recv_sem.at[h, stage, k - 1],
            device_id=device(*other, core), device_id_type=MESH,
        )

    def to_sibling(h, k):
        part = region(h, 2, lax.rem(at[h][2] + 4 - k, 4))
        return pltpu.make_async_remote_copy(
            src_ref=part, dst_ref=part, send_sem=sib_send.at[h, k], recv_sem=sib_recv.at[h, k],
            device_id=device(x, y, z, 1 - core), device_id_type=MESH,
        )

    def halo(k):
        return pltpu.make_async_remote_copy(
            src_ref=window.at[pl.ds(256, 256), :], dst_ref=window.at[pl.ds(512 * k, 256), :],
            send_sem=halo_send.at[k], recv_sem=halo_recv.at[k], device_id=(after, before)[k], device_id_type=MESH,
        )

    hops = [(h, k) for k in (1, 3, 2) for h in range(2)]

    for c in lists[:3]:
        c.wait()
    place = src_v[...] - (me - 1) * TARGETS
    slot = lax.broadcasted_iota(jnp.int32, (SLOTS, TARGETS), 0)
    joint = jnp.where(slot < count_v[...], lax.shift_right_arithmetic(place, 8) * NOPS + op_v[...], -1)
    tmp[...] = jnp.full((256, 256), -1.0, F32)
    tmp[:SLOTS, :] = joint.astype(F32)
    slot_q[...] = tmp[...].T
    tmp[:SLOTS, :] = (place & 255).astype(F32)
    slot_c[...] = tmp[...].T

    for c in own + [mid]:
        c.wait()
    pl.semaphore_wait(barrier, len(partners))
    for h, k in hops:
        hop(h, 0, k).start()
    halo(0).start()
    halo(1).start()

    for c in lists[3:]:
        c.wait()
    tmp[:128, :] = jnp.full((128, 256), -1.0, F32)
    tmp[:COARSE_SLOTS, :] = cop_v[...].astype(F32)
    slot_cop[...] = tmp[:128, :].T
    picked0[...] = jnp.zeros_like(picked0)
    picked1[...] = jnp.zeros_like(picked1)

    def count_slots(i, _):
        @pl.when(i == 3)
        def _():
            for h, k in hops:
                hop(h, 0, k).wait_recv()
            for h, k in hops:
                hop(h, 1, k).start()

        @pl.when(i == 8)
        def _():
            for h, k in hops:
                hop(h, 1, k).wait_recv()
            for h, k in hops:
                hop(h, 2, k).start()
            for h in range(2):
                to_sibling(h, 0).start()

        for u in range(STEP):
            t = i * STEP + u
            q = jnp.broadcast_to(slot_q[pl.ds(t, 1), :], (16, 256)).astype(BF16)
            c = jnp.broadcast_to(slot_c[pl.ds(t, 1), :], (16, 256)).astype(BF16)
            hot_q = one_hot_rows(q, 9).astype(F8)
            hot_c = one_hot_rows(c, 16).astype(F8)
            n = lax.dot_general(hot_q, hot_c, LAST, preferred_element_type=F32).astype(BF16)
            for s in range(3):
                tally[s, pl.ds(pl.multiple_of(t * NOPS, NOPS), NOPS), :] = n[s * NOPS : (s + 1) * NOPS]
        return 0

    lax.fori_loop(0, TARGETS // STEP, count_slots, 0)

    for k in (1, 3, 2):
        for h in range(2):
            hop(h, 2, k).wait_recv()
            to_sibling(h, k).start()
    for k in range(2):
        halo(k).wait_recv()
    for k in (0, 1, 3, 2):
        for h in range(2):
            to_sibling(h, k).wait_recv()

    def fill(i, _):
        cx, cy, cz = lax.div(i, 16), lax.rem(lax.div(i, 4), 4), lax.rem(i, 4)
        chip = (cx, cy, cz)
        for f in range(4):
            a, b, c = (chip[ORDERS[f][s]] for s in range(3))
            v = received[f, pl.ds(pl.multiple_of((c * 16 + b * 4 + a) * 16, 16), 16), :].astype(F32)
            row = pl.ds(pl.multiple_of(i * 64 + f * 16, 16), 16)
            table[row, 0, :] = v[:, :128]
            table[row, 1, :] = v[:, 128:]
        return 0

    lax.fori_loop(0, 64, fill, 0)

    number = lax.broadcasted_iota(jnp.int32, (NOPS, 32), 0).astype(F32)

    def gather(t0, picked):
        for u in range(STEP):
            for j in range(COARSE_SLOTS):
                picked[pl.ds((u * 32 + j) * 2, 2), :] = table[csrc[j, t0 + u]]

    def groups(t0, picked):
        rows = pl.ds(pl.multiple_of(t0 * NOPS, STEP * NOPS), STEP * NOPS)
        near = jnp.zeros((STEP * NOPS, COEFFS), F32)
        for s in range(3):
            near = near + jnp.dot(tally[s, rows, :], window[s * 256 : (s + 1) * 256, :], preferred_element_type=F32)
        total = []
        for u in range(STEP):
            lo = picked[pl.ds(u * 64, 32, stride=2), :].astype(BF16)
            hi = picked[pl.ds(u * 64 + 1, 32, stride=2), :].astype(BF16)
            o = jnp.broadcast_to(slot_cop[pl.ds(t0 + u, 1), :32], (NOPS, 32))
            hot = jnp.where(o == number, 1.0, 0.0).astype(BF16)
            far = jnp.dot(hot, jnp.concatenate([lo, hi], axis=1), preferred_element_type=F32)
            total.append(near[u * NOPS : (u + 1) * NOPS] + far)
        for r in range(0, NOPS, 8):
            parts = [transpose8([total[p * 8 + k][r : r + 8] for k in range(8)]) for p in range(STEP // 8)]
            for k in range(8):
                group[r + k, pl.ds(pl.multiple_of(t0, STEP), STEP), :] = jnp.concatenate(
                    [p[k] for p in parts], axis=0
                ).astype(BF16)

    gather(0, picked0)

    def two(i, _):
        t0 = i * (2 * STEP)
        gather(t0 + STEP, picked1)
        groups(t0, picked0)
        gather(jnp.minimum(t0 + 2 * STEP, TARGETS - STEP), picked0)
        groups(t0 + STEP, picked1)
        return 0

    lax.fori_loop(0, TARGETS // (2 * STEP), two, 0)

    weights.wait()
    out[...] = jnp.zeros_like(out)

    def translate(i, _):
        acc = out[...]
        for u in range(4):
            r = i * 4 + u
            acc = acc + lax.dot_general(group[r], ops[r], LAST, preferred_element_type=F32)
        out[...] = acc
        return 0

    lax.fori_loop(0, NOPS // 4, translate, 0)

    for stage in range(3):
        for h, k in hops:
            hop(h, stage, k).wait_send()
    for k in range(4):
        for h in range(2):
            to_sibling(h, k).wait_send()
    for k in range(2):
        halo(k).wait_send()


def local(
    multipole, coarse_multipole, operators, source_list, op_list, list_count, coarse_src, coarse_op
):
    here = pl.BlockSpec(memory_space=pl.ANY)
    vmem = pltpu.VMEM
    return pl.pallas_call(
        kernel,
        out_shape=jax.ShapeDtypeStruct((TARGETS, COEFFS), F32),
        in_specs=[here] * 8,
        out_specs=pl.BlockSpec(memory_space=vmem),
        scratch_shapes=[
            vmem((3 * 256, 256), BF16),
            vmem((4, 1024, 256), BF16),
            vmem((4096, 2, 128), F32),
            vmem((NOPS, 256, 256), BF16),
            vmem((SLOTS, 256), jnp.int32),
            vmem((SLOTS, 256), jnp.int32),
            vmem((1, 256), jnp.int32),
            vmem((COARSE_SLOTS, 256), jnp.int32),
            pltpu.SMEM((COARSE_SLOTS, 256), jnp.int32),
            vmem((256, 256), F32),
            vmem((256, 256), F32),
            vmem((256, 128), F32),
            vmem((256, 256), F32),
            vmem((3, TARGETS * NOPS, 256), BF16),
            vmem((STEP * 64, 128), F32),
            vmem((STEP * 64, 128), F32),
            vmem((NOPS, TARGETS, COEFFS), BF16),
            pltpu.SemaphoreType.DMA((9,)),
            pltpu.SemaphoreType.DMA((2, 3, 3)),
            pltpu.SemaphoreType.DMA((2, 3, 3)),
            pltpu.SemaphoreType.DMA((2, 4)),
            pltpu.SemaphoreType.DMA((2, 4)),
            pltpu.SemaphoreType.DMA((2,)),
            pltpu.SemaphoreType.DMA((2,)),
        ],
        compiler_params=pltpu.CompilerParams(
            collective_id=0, has_side_effects=True, vmem_limit_bytes=60 * 1024 * 1024
        ),
        cost_estimate=pl.CostEstimate(flops=14_000_000_000, bytes_accessed=12_000_000, transcendentals=0),
    )(
        multipole, coarse_multipole, operators, source_list.T, op_list.T, list_count.reshape(1, TARGETS),
        coarse_src.T, coarse_op.T,
    )


def solution(mesh):
    blocks = P(("gx", "gy"), None)
    placed = (blocks, blocks, P(), blocks, blocks, P(("gx", "gy")), blocks, blocks)
    return jax.shard_map(local, mesh=mesh, in_specs=placed, out_specs=blocks, check_vma=False)
```

```python
import functools

import jax
import jax.numpy as jnp
from jax import lax
from jax.experimental import pallas as pl
from jax.experimental.pallas import tpu as pltpu
from jax.sharding import PartitionSpec as P

TARGETS = 256
SLOTS = 189
COARSE_SLOTS = 27
NOPS = 48
COEFFS = 256
STEP = 16
RING = 4
F8 = jnp.float8_e4m3fn
BF16 = jnp.bfloat16
F32 = jnp.float32
LAST = (((1,), (1,)), ((), ()))
MESH = pl.DeviceIdType.MESH

ORDERS = ((2, 1, 0), (0, 2, 1), (1, 0, 2), (2, 1, 0))


def one_hot_rows(row, blocks):
    number = lax.broadcasted_iota(jnp.int32, row.shape, 0).astype(F32)
    one, zero = BF16(1), BF16(0)
    return jnp.concatenate(
        [jnp.where(row == (number + 16.0 * k).astype(BF16), one, zero) for k in range(blocks)], axis=0
    )


def transpose8(v):
    row = lax.broadcasted_iota(jnp.int32, v[0].shape, 0)
    cur = [v[0]] + [pltpu.roll(v[k], k, 0) for k in range(1, 8)]
    for bit in (1, 2, 4):
        odd = (row & bit) != 0
        cur = [jnp.where(odd, cur[(k + bit) % 8], cur[k]) for k in range(8)]
    return [cur[0]] + [pltpu.roll(cur[8 - r], 8 - r, 0) for r in range(1, 8)]


def kernel(
    multipole, coarse, operators, source_t, op_t, count, coarse_src_t, coarse_op_t,
    out,
    window, received, table, ops, src_v, op_v, count_v, cop_v, csrc_v, index_v, index_s, slot_q, slot_c, slot_cop, cop_rows, tmp, tmp_i, tally, near, picked0, picked1, group,
    local_sem, index_sem, send_sem, recv_sem, sib_send, sib_recv, halo_send, halo_recv,
):
    x = lax.axis_index("gx")
    gy = lax.axis_index("gy")
    y, z, core = lax.div(gy, 8), lax.rem(lax.div(gy, 2), 4), lax.rem(gy, 2)
    coords = (x, y, z)
    me = x * 32 + gy

    def device(cx, cy, cz, cc):
        return (cx, (cy * 4 + cz) * 2 + cc)

    def linear(d):
        return (lax.div(d, 32), lax.rem(d, 32))

    def local(src, dst, k):
        return pltpu.make_async_copy(src, dst, local_sem.at[k])

    rows16 = lambda f, pos, n: received.at[f, pl.ds(pl.multiple_of(pos * 16, 16), n * 16), :]
    flow = [core * 2 + h for h in range(2)]
    at = []
    for h in range(2):
        at.append([coords[ORDERS[h][s]] * (1 - core) + coords[ORDERS[2 + h][s]] * core for s in range(3)])

    def region(h, stage, last=None):
        a, b, c = at[h]
        c = c if last is None else last
        if stage == 0:
            return rows16(flow[h], c * 16 + b * 4 + a, 1)
        if stage == 1:
            return rows16(flow[h], c * 16 + b * 4, 4)
        return rows16(flow[h], c * 16, 16)

    own = [local(coarse.at[pl.ds(h * 16, 16), :], region(h, 0), h) for h in range(2)]
    mid = local(multipole, window.at[pl.ds(256, 256), :], 2)
    lists = [
        local(source_t, src_v, 3), local(op_t, op_v, 4), local(count, count_v, 5), local(coarse_op_t, cop_v, 6),
        local(coarse_src_t, csrc_v, 7),
    ]
    weights = local(operators, ops, 8)
    for c in own + [mid] + lists + [weights]:
        c.start()

    barrier = pltpu.get_barrier_semaphore()
    after, before = linear(lax.rem(me + 1, 128)), linear(lax.rem(me + 127, 128))
    partners = [device(x, y, z, 1 - core), after, before]
    for axis in range(3):
        for k in range(1, 4):
            other = list(coords)
            other[axis] = lax.rem(coords[axis] + k, 4)
            partners.append(device(*other, core))
    for p in partners:
        pl.semaphore_signal(barrier, inc=1, device_id=p, device_id_type=MESH)

    def hop(h, stage, k):
        other = list(coords)
        for c, weight in ((0, 1 - core), (1, core)):
            axis = ORDERS[2 * c + h][stage]
            other[axis] = other[axis] + weight * (lax.rem(coords[axis] + k, 4) - coords[axis])
        part = region(h, stage)
        return pltpu.make_async_remote_copy(
            src_ref=part, dst_ref=part, send_sem=send_sem.at[h, stage, k - 1], recv_sem=recv_sem.at[h, stage, k - 1],
            device_id=device(*other, core), device_id_type=MESH,
        )

    def to_sibling(h, k):
        part = region(h, 2, lax.rem(at[h][2] + 4 - k, 4))
        return pltpu.make_async_remote_copy(
            src_ref=part, dst_ref=part, send_sem=sib_send.at[h, k], recv_sem=sib_recv.at[h, k],
            device_id=device(x, y, z, 1 - core), device_id_type=MESH,
        )

    def halo(k):
        return pltpu.make_async_remote_copy(
            src_ref=window.at[pl.ds(256, 256), :], dst_ref=window.at[pl.ds(512 * k, 256), :],
            send_sem=halo_send.at[k], recv_sem=halo_recv.at[k], device_id=(after, before)[k], device_id_type=MESH,
        )

    hops = [(h, k) for k in (1, 3, 2) for h in range(2)]

    for c in own + [mid]:
        c.wait()
    pl.semaphore_wait(barrier, len(partners))
    for h, k in hops:
        hop(h, 0, k).start()
    halo(0).start()
    halo(1).start()

    for c in lists[:3]:
        c.wait()
    place = src_v[...] - (me - 1) * TARGETS
    slot = lax.broadcasted_iota(jnp.int32, (SLOTS, TARGETS), 0)
    joint = jnp.where(slot < count_v[...], lax.shift_right_arithmetic(place, 8) * NOPS + op_v[...], -1)
    tmp[...] = jnp.full((256, 256), -1.0, F32)
    tmp[:SLOTS, :] = joint.astype(F32)
    slot_q[...] = tmp[...].T
    tmp[:SLOTS, :] = (place & 255).astype(F32)
    slot_c[...] = tmp[...].T

    for c in lists[3:]:
        c.wait()
    tmp[:128, :] = jnp.full((128, 256), -1.0, F32)
    tmp[:COARSE_SLOTS, :] = cop_v[...].astype(F32)
    slot_cop[...] = tmp[:128, :].T
    for u in range(8):
        cop_rows[:, u * 32 : (u + 1) * 32] = slot_cop[pl.ds(u, TARGETS // 8, stride=8), :][:, :32]
    tmp_i[...] = jnp.zeros_like(tmp_i)
    tmp_i[:COARSE_SLOTS, :] = csrc_v[...]
    index_v[...] = tmp_i[...].T
    picked0[...] = jnp.zeros_like(picked0)
    picked1[...] = jnp.zeros_like(picked1)

    def fetch(pair, k):
        return pltpu.make_async_copy(
            index_v.at[pl.ds(pl.multiple_of(pair * STEP, STEP), STEP), :], index_s.at[k], index_sem.at[k]
        )

    for k in range(RING):
        fetch(k, k).start()

    def count_slots(i, _):
        @pl.when(i == 6)
        def _():
            for h, k in hops:
                hop(h, 0, k).wait_recv()
            for h, k in hops:
                hop(h, 1, k).start()

        @pl.when(i == 12)
        def _():
            for h, k in hops:
                hop(h, 1, k).wait_recv()
            for h, k in hops:
                hop(h, 2, k).start()
            for h in range(2):
                to_sibling(h, 0).start()

        for u in range(STEP):
            t = i * STEP + u
            q = jnp.broadcast_to(slot_q[pl.ds(t, 1), :], (16, 256)).astype(BF16)
            c = jnp.broadcast_to(slot_c[pl.ds(t, 1), :], (16, 256)).astype(BF16)
            hot_q = one_hot_rows(q, 9).astype(F8)
            hot_c = one_hot_rows(c, 16).astype(F8)
            n = lax.dot_general(hot_q, hot_c, LAST, preferred_element_type=F32).astype(BF16)
            for s in range(3):
                tally[s, pl.ds(pl.multiple_of(t * NOPS, NOPS), NOPS), :] = n[s * NOPS : (s + 1) * NOPS]
        return 0

    lax.fori_loop(0, TARGETS // STEP, count_slots, 0)

    for k in range(2):
        halo(k).wait_recv()

    def near_groups(i, _):
        @pl.when(i == 10)
        def _():
            for k in (1, 3, 2):
                for h in range(2):
                    hop(h, 2, k).wait_recv()
                    to_sibling(h, k).start()

        t0 = i * STEP
        rows = pl.ds(pl.multiple_of(t0 * NOPS, STEP * NOPS), STEP * NOPS)
        acc = jnp.zeros((STEP * NOPS, COEFFS), F32)
        for s in range(3):
            acc = acc + jnp.dot(tally[s, rows, :], window[s * 256 : (s + 1) * 256, :], preferred_element_type=F32)
        for r in range(0, NOPS, 8):
            for p in range(STEP // 8):
                first = [(p * 8 + k) * NOPS + r for k in range(8)]
                turned = transpose8([acc[a : a + 8] for a in first])
                for k in range(8):
                    near[r + k, pl.ds(pl.multiple_of(t0 + 8 * p, 8), 8), :] = turned[k]
        return 0

    lax.fori_loop(0, TARGETS // STEP, near_groups, 0)

    def fill(cc):
        def chip(i, _):
            at_chip = (lax.div(i, 16), lax.rem(lax.div(i, 4), 4), lax.rem(i, 4))
            for h in range(2):
                a, b, c = (
                    at_chip[ORDERS[h][s]] * (1 - cc) + at_chip[ORDERS[2 + h][s]] * cc for s in range(3)
                )
                v = received[cc * 2 + h, pl.ds(pl.multiple_of((c * 16 + b * 4 + a) * 16, 16), 16), :].astype(F32)
                row = pl.ds(pl.multiple_of(i * 64 + cc * 32 + h * 16, 16), 16)
                table[row, 0, :] = v[:, :128]
                table[row, 1, :] = v[:, 128:]
            return 0

        lax.fori_loop(0, 64, chip, 0)

    fill(core)
    for k in (0, 1, 3, 2):
        for h in range(2):
            to_sibling(h, k).wait_recv()
    fill(1 - core)

    row_no = lax.broadcasted_iota(jnp.int32, (16, 256), 0)
    same = (row_no & 7) == lax.shift_right_logical(lax.broadcasted_iota(jnp.int32, (16, 256), 1), 5)
    number = lax.shift_right_logical(row_no, 3).astype(F32)

    def gather(k, picked):
        for u in range(STEP):
            for j in range(COARSE_SLOTS):
                picked[pl.ds((u * 32 + j) * 2, 2), :] = table[index_s[k, u, j]]

    def far(eight, picked, p):
        lo = picked[pl.ds(512 * p, 256, stride=2), :].astype(BF16)
        hi = picked[pl.ds(512 * p + 1, 256, stride=2), :].astype(BF16)
        o = jnp.broadcast_to(cop_rows[pl.ds(eight, 1), :], (16, 256))
        o = jnp.where(same, o, -1.0).astype(BF16)
        hot = jnp.concatenate(
            [jnp.where(o == (number + 2.0 * k).astype(BF16), BF16(1), BF16(0)) for k in range(NOPS // 2)], axis=0
        )
        return jnp.dot(hot, jnp.concatenate([lo, hi], axis=1), preferred_element_type=F32)

    picked = (picked0, picked1)
    pairs = TARGETS // STEP
    fetch(0, 0).wait()
    gather(0, picked0)
    fetch(RING, 0).start()

    def coarse_groups(i, _):
        for k in range(RING):
            pair, nxt = i * RING + k, (k + 1) % RING
            fetch(0, nxt).wait()
            gather(nxt, picked[(k + 1) % 2])
            fetch(jnp.minimum(pair + 1 + RING, pairs - 1), nxt).start()
            f0, f1 = far(2 * pair, picked[k % 2], 0), far(2 * pair + 1, picked[k % 2], 1)
            at_t = pl.ds(pl.multiple_of(pair * STEP, STEP), STEP)
            for r in range(NOPS):
                both = jnp.concatenate([f0[r * 8 : r * 8 + 8], f1[r * 8 : r * 8 + 8]], axis=0)
                group[r, at_t, :] = (near[r, at_t, :] + both).astype(BF16)
        return 0

    lax.fori_loop(0, pairs // RING, coarse_groups, 0)
    for k in range(RING):
        fetch(0, k).wait()

    weights.wait()
    out[...] = jnp.zeros_like(out)

    def translate(i, _):
        acc = out[...]
        for u in range(16):
            r = i * 16 + u
            acc = acc + lax.dot_general(group[r], ops[r], LAST, preferred_element_type=F32)
        out[...] = acc
        return 0

    lax.fori_loop(0, NOPS // 16, translate, 0)

    for stage in range(3):
        for h, k in hops:
            hop(h, stage, k).wait_send()
    for k in range(4):
        for h in range(2):
            to_sibling(h, k).wait_send()
    for k in range(2):
        halo(k).wait_send()


def local(
    multipole, coarse_multipole, operators, source_list, op_list, list_count, coarse_src, coarse_op
):
    here = pl.BlockSpec(memory_space=pl.ANY)
    vmem = pltpu.VMEM
    return pl.pallas_call(
        kernel,
        out_shape=vmem((TARGETS, COEFFS), F32),
        in_specs=[here] * 8,
        out_specs=pl.BlockSpec(memory_space=vmem),
        scratch_shapes=[
            vmem((3 * 256, 256), BF16),
            vmem((4, 1024, 256), BF16),
            vmem((4096, 2, 128), F32),
            vmem((NOPS, 256, 256), BF16),
            vmem((SLOTS, 256), jnp.int32),
            vmem((SLOTS, 256), jnp.int32),
            vmem((1, 256), jnp.int32),
            vmem((COARSE_SLOTS, 256), jnp.int32),
            vmem((COARSE_SLOTS, 256), jnp.int32),
            vmem((256, 128), jnp.int32),
            pltpu.SMEM((RING, STEP, 128), jnp.int32),
            vmem((256, 256), F32),
            vmem((256, 256), F32),
            vmem((256, 128), F32),
            vmem((TARGETS // 8, 256), F32),
            vmem((256, 256), F32),
            vmem((128, 256), jnp.int32),
            vmem((3, TARGETS * NOPS, 256), BF16),
            vmem((NOPS, TARGETS, COEFFS), F32),
            vmem((STEP * 64, 128), F32),
            vmem((STEP * 64, 128), F32),
            vmem((NOPS, TARGETS, COEFFS), BF16),
            pltpu.SemaphoreType.DMA((9,)),
            pltpu.SemaphoreType.DMA((RING,)),
            pltpu.SemaphoreType.DMA((2, 3, 3)),
            pltpu.SemaphoreType.DMA((2, 3, 3)),
            pltpu.SemaphoreType.DMA((2, 4)),
            pltpu.SemaphoreType.DMA((2, 4)),
            pltpu.SemaphoreType.DMA((2,)),
            pltpu.SemaphoreType.DMA((2,)),
        ],
        compiler_params=pltpu.CompilerParams(
            collective_id=0, has_side_effects=True, vmem_limit_bytes=60 * 1024 * 1024
        ),
        cost_estimate=pl.CostEstimate(flops=14_000_000_000, bytes_accessed=12_000_000, transcendentals=0),
    )(
        multipole, coarse_multipole, operators, source_list.T, op_list.T, list_count.reshape(1, TARGETS),
        coarse_src.T, coarse_op.T,
    )


def solution(mesh):
    blocks = P(("gx", "gy"), None)
    placed = (blocks, blocks, P(), blocks, blocks, P(("gx", "gy")), blocks, blocks)
    return jax.shard_map(local, mesh=mesh, in_specs=placed, out_specs=blocks, check_vma=False)
```

```python
import functools

import jax
import jax.numpy as jnp
from jax import lax
from jax.experimental import pallas as pl
from jax.experimental.pallas import tpu as pltpu
from jax.sharding import PartitionSpec as P

TARGETS = 256
SLOTS = 189
COARSE_SLOTS = 27
NOPS = 48
COEFFS = 256
STEP = 16
RING = 4
F8 = jnp.float8_e4m3fn
BF16 = jnp.bfloat16
F32 = jnp.float32
LAST = (((1,), (1,)), ((), ()))
MESH = pl.DeviceIdType.MESH

ORDERS = ((2, 1, 0), (0, 2, 1), (1, 0, 2), (2, 1, 0))


def one_hot_rows(row, blocks):
    number = lax.broadcasted_iota(jnp.int32, row.shape, 0).astype(F32)
    one, zero = BF16(1), BF16(0)
    return jnp.concatenate(
        [jnp.where(row == (number + 16.0 * k).astype(BF16), one, zero) for k in range(blocks)], axis=0
    )


def transpose8(v):
    row = lax.broadcasted_iota(jnp.int32, v[0].shape, 0)
    cur = [v[0]] + [pltpu.roll(v[k], k, 0) for k in range(1, 8)]
    for bit in (1, 2, 4):
        odd = (row & bit) != 0
        cur = [jnp.where(odd, cur[(k + bit) % 8], cur[k]) for k in range(8)]
    return [cur[0]] + [pltpu.roll(cur[8 - r], 8 - r, 0) for r in range(1, 8)]


def kernel(
    multipole, coarse, operators, source_t, op_t, count, coarse_src_t, coarse_op_t,
    out,
    window, received, table, ops, src_v, op_v, count_v, cop_v, csrc_v, index_v, index_s, slot_q, slot_c, slot_cop, cop_rows, tmp, tmp_i, tally, near, picked0, picked1, group,
    local_sem, index_sem, send_sem, recv_sem, sib_send, sib_recv, halo_send, halo_recv,
):
    x = lax.axis_index("gx")
    gy = lax.axis_index("gy")
    y, z, core = lax.div(gy, 8), lax.rem(lax.div(gy, 2), 4), lax.rem(gy, 2)
    coords = (x, y, z)
    me = x * 32 + gy

    def device(cx, cy, cz, cc):
        return (cx, (cy * 4 + cz) * 2 + cc)

    def linear(d):
        return (lax.div(d, 32), lax.rem(d, 32))

    def local(src, dst, k):
        return pltpu.make_async_copy(src, dst, local_sem.at[k])

    rows16 = lambda f, pos, n: received.at[f, pl.ds(pl.multiple_of(pos * 16, 16), n * 16), :]
    flow = [core * 2 + h for h in range(2)]
    at = []
    for h in range(2):
        at.append([coords[ORDERS[h][s]] * (1 - core) + coords[ORDERS[2 + h][s]] * core for s in range(3)])

    def region(h, stage, last=None):
        a, b, c = at[h]
        c = c if last is None else last
        if stage == 0:
            return rows16(flow[h], c * 16 + b * 4 + a, 1)
        if stage == 1:
            return rows16(flow[h], c * 16 + b * 4, 4)
        return rows16(flow[h], c * 16, 16)

    own = [local(coarse.at[pl.ds(h * 16, 16), :], region(h, 0), h) for h in range(2)]
    mid = local(multipole, window.at[pl.ds(256, 256), :], 2)
    lists = [
        local(source_t, src_v, 3), local(op_t, op_v, 4), local(count, count_v, 5), local(coarse_op_t, cop_v, 6),
        local(coarse_src_t, csrc_v, 7),
    ]
    weights = local(operators, ops, 8)
    for c in own + [mid] + lists + [weights]:
        c.start()

    barrier = pltpu.get_barrier_semaphore()
    after, before = linear(lax.rem(me + 1, 128)), linear(lax.rem(me + 127, 128))
    partners = [device(x, y, z, 1 - core), after, before]
    for axis in range(3):
        for k in range(1, 4):
            other = list(coords)
            other[axis] = lax.rem(coords[axis] + k, 4)
            partners.append(device(*other, core))
    for p in partners:
        pl.semaphore_signal(barrier, inc=1, device_id=p, device_id_type=MESH)

    def hop(h, stage, k):
        other = list(coords)
        for c, weight in ((0, 1 - core), (1, core)):
            axis = ORDERS[2 * c + h][stage]
            other[axis] = other[axis] + weight * (lax.rem(coords[axis] + k, 4) - coords[axis])
        part = region(h, stage)
        return pltpu.make_async_remote_copy(
            src_ref=part, dst_ref=part, send_sem=send_sem.at[h, stage, k - 1], recv_sem=recv_sem.at[h, stage, k - 1],
            device_id=device(*other, core), device_id_type=MESH,
        )

    def to_sibling(h, k):
        part = region(h, 2, lax.rem(at[h][2] + 4 - k, 4))
        return pltpu.make_async_remote_copy(
            src_ref=part, dst_ref=part, send_sem=sib_send.at[h, k], recv_sem=sib_recv.at[h, k],
            device_id=device(x, y, z, 1 - core), device_id_type=MESH,
        )

    def halo(k):
        return pltpu.make_async_remote_copy(
            src_ref=window.at[pl.ds(256, 256), :], dst_ref=window.at[pl.ds(512 * k, 256), :],
            send_sem=halo_send.at[k], recv_sem=halo_recv.at[k], device_id=(after, before)[k], device_id_type=MESH,
        )

    hops = [(h, k) for k in (1, 3, 2) for h in range(2)]

    for c in lists[:3]:
        c.wait()
    place = src_v[...] - (me - 1) * TARGETS
    slot = lax.broadcasted_iota(jnp.int32, (SLOTS, TARGETS), 0)
    joint = jnp.where(slot < count_v[...], lax.shift_right_arithmetic(place, 8) * NOPS + op_v[...], -1)
    tmp[...] = jnp.full((256, 256), -1.0, F32)
    tmp[:SLOTS, :] = joint.astype(F32)
    slot_q[...] = tmp[...].T
    tmp[:SLOTS, :] = (place & 255).astype(F32)
    slot_c[...] = tmp[...].T

    for c in lists[3:]:
        c.wait()
    tmp[:128, :] = jnp.full((128, 256), -1.0, F32)
    tmp[:COARSE_SLOTS, :] = cop_v[...].astype(F32)
    slot_cop[...] = tmp[:128, :].T
    for u in range(8):
        cop_rows[:, u * 32 : (u + 1) * 32] = slot_cop[pl.ds(u, TARGETS // 8, stride=8), :][:, :32]
    tmp_i[...] = jnp.zeros_like(tmp_i)
    tmp_i[:COARSE_SLOTS, :] = csrc_v[...]
    index_v[...] = tmp_i[...].T
    picked0[...] = jnp.zeros_like(picked0)
    picked1[...] = jnp.zeros_like(picked1)

    def fetch(pair, k):
        return pltpu.make_async_copy(
            index_v.at[pl.ds(pl.multiple_of(pair * STEP, STEP), STEP), :], index_s.at[k], index_sem.at[k]
        )

    for k in range(RING):
        fetch(k, k).start()

    def count_slots(i, _):
        @pl.when(i == 4)
        def _():
            for c in own + [mid]:
                c.wait()
            pl.semaphore_wait(barrier, len(partners))
            for h, k in hops:
                hop(h, 0, k).start()
            halo(0).start()
            halo(1).start()

        @pl.when(i == 10)
        def _():
            for h, k in hops:
                hop(h, 0, k).wait_recv()
            for h, k in hops:
                hop(h, 1, k).start()

        @pl.when(i == 15)
        def _():
            for h, k in hops:
                hop(h, 1, k).wait_recv()
            for h, k in hops:
                hop(h, 2, k).start()
            for h in range(2):
                to_sibling(h, 0).start()

        for u in range(STEP):
            t = i * STEP + u
            q = jnp.broadcast_to(slot_q[pl.ds(t, 1), :], (16, 256)).astype(BF16)
            c = jnp.broadcast_to(slot_c[pl.ds(t, 1), :], (16, 256)).astype(BF16)
            hot_q = one_hot_rows(q, 9).astype(F8)
            hot_c = one_hot_rows(c, 16).astype(F8)
            n = lax.dot_general(hot_q, hot_c, LAST, preferred_element_type=F32).astype(BF16)
            for s in range(3):
                tally[s, pl.ds(pl.multiple_of(t * NOPS, NOPS), NOPS), :] = n[s * NOPS : (s + 1) * NOPS]
        return 0

    lax.fori_loop(0, TARGETS // STEP, count_slots, 0)

    for k in range(2):
        halo(k).wait_recv()

    def near_groups(i, _):
        @pl.when(i == 13)
        def _():
            for k in (1, 3, 2):
                for h in range(2):
                    hop(h, 2, k).wait_recv()
                    to_sibling(h, k).start()

        t0 = i * STEP
        rows = pl.ds(pl.multiple_of(t0 * NOPS, STEP * NOPS), STEP * NOPS)
        acc = jnp.zeros((STEP * NOPS, COEFFS), F32)
        for s in range(3):
            acc = acc + jnp.dot(tally[s, rows, :], window[s * 256 : (s + 1) * 256, :], preferred_element_type=F32)
        for r in range(0, NOPS, 8):
            for p in range(STEP // 8):
                first = [(p * 8 + k) * NOPS + r for k in range(8)]
                turned = transpose8([acc[a : a + 8] for a in first])
                for k in range(8):
                    near[r + k, pl.ds(pl.multiple_of(t0 + 8 * p, 8), 8), :] = turned[k]
        return 0

    lax.fori_loop(0, TARGETS // STEP, near_groups, 0)

    def fill(cc, last):
        scale = [
            [4 ** (2 - ORDERS[h][s]) * (1 - cc) + 4 ** (2 - ORDERS[2 + h][s]) * cc for s in range(3)] for h in range(2)
        ]

        def chip(i, _):
            b, a = lax.div(i, 4), lax.rem(i, 4)
            for h in range(2):
                v = received[cc * 2 + h, pl.ds(pl.multiple_of((last[h] * 16 + i) * 16, 16), 16), :].astype(F32)
                place = a * scale[h][0] + b * scale[h][1] + last[h] * scale[h][2]
                row = pl.ds(pl.multiple_of(place * 64 + cc * 32 + h * 16, 16), 16)
                table[row, 0, :] = v[:, :128]
                table[row, 1, :] = v[:, 128:]
            return 0

        lax.fori_loop(0, 16, chip, 0)

    for k in range(4):
        fill(core, [lax.rem(at[h][2] + 4 - k, 4) for h in range(2)])
    beside = [coords[ORDERS[h][2]] * core + coords[ORDERS[2 + h][2]] * (1 - core) for h in range(2)]
    for k in (0, 1, 3, 2):
        for h in range(2):
            to_sibling(h, k).wait_recv()
        fill(1 - core, [lax.rem(beside[h] + 4 - k, 4) for h in range(2)])

    row_no = lax.broadcasted_iota(jnp.int32, (16, 256), 0)
    same = (row_no & 7) == lax.shift_right_logical(lax.broadcasted_iota(jnp.int32, (16, 256), 1), 5)
    number = lax.shift_right_logical(row_no, 3).astype(F32)

    def gather(k, picked):
        for u in range(STEP):
            for j in range(COARSE_SLOTS):
                picked[pl.ds((u * 32 + j) * 2, 2), :] = table[index_s[k, u, j]]

    def far(eight, picked, p):
        lo = picked[pl.ds(512 * p, 256, stride=2), :].astype(BF16)
        hi = picked[pl.ds(512 * p + 1, 256, stride=2), :].astype(BF16)
        o = jnp.broadcast_to(cop_rows[pl.ds(eight, 1), :], (16, 256))
        o = jnp.where(same, o, -1.0).astype(BF16)
        hot = jnp.concatenate(
            [jnp.where(o == (number + 2.0 * k).astype(BF16), BF16(1), BF16(0)) for k in range(NOPS // 2)], axis=0
        )
        return jnp.dot(hot, jnp.concatenate([lo, hi], axis=1), preferred_element_type=F32)

    picked = (picked0, picked1)
    pairs = TARGETS // STEP
    fetch(0, 0).wait()
    gather(0, picked0)
    fetch(RING, 0).start()

    def coarse_groups(i, _):
        for k in range(RING):
            pair, nxt = i * RING + k, (k + 1) % RING
            fetch(0, nxt).wait()
            gather(nxt, picked[(k + 1) % 2])
            fetch(jnp.minimum(pair + 1 + RING, pairs - 1), nxt).start()
            f0, f1 = far(2 * pair, picked[k % 2], 0), far(2 * pair + 1, picked[k % 2], 1)
            at_t = pl.ds(pl.multiple_of(pair * STEP, STEP), STEP)
            for r in range(NOPS):
                both = jnp.concatenate([f0[r * 8 : r * 8 + 8], f1[r * 8 : r * 8 + 8]], axis=0)
                group[r, at_t, :] = (near[r, at_t, :] + both).astype(BF16)
        return 0

    lax.fori_loop(0, pairs // RING, coarse_groups, 0)
    for k in range(RING):
        fetch(0, k).wait()

    weights.wait()
    out[...] = jnp.zeros_like(out)

    def translate(i, _):
        acc = out[...]
        for u in range(16):
            r = i * 16 + u
            acc = acc + lax.dot_general(group[r], ops[r], LAST, preferred_element_type=F32)
        out[...] = acc
        return 0

    lax.fori_loop(0, NOPS // 16, translate, 0)

    for stage in range(3):
        for h, k in hops:
            hop(h, stage, k).wait_send()
    for k in range(4):
        for h in range(2):
            to_sibling(h, k).wait_send()
    for k in range(2):
        halo(k).wait_send()


def local(
    multipole, coarse_multipole, operators, source_list, op_list, list_count, coarse_src, coarse_op
):
    here = pl.BlockSpec(memory_space=pl.ANY)
    vmem = pltpu.VMEM
    return pl.pallas_call(
        kernel,
        out_shape=vmem((TARGETS, COEFFS), F32),
        in_specs=[here] * 8,
        out_specs=pl.BlockSpec(memory_space=vmem),
        scratch_shapes=[
            vmem((3 * 256, 256), BF16),
            vmem((4, 1024, 256), BF16),
            vmem((4096, 2, 128), F32),
            vmem((NOPS, 256, 256), BF16),
            vmem((SLOTS, 256), jnp.int32),
            vmem((SLOTS, 256), jnp.int32),
            vmem((1, 256), jnp.int32),
            vmem((COARSE_SLOTS, 256), jnp.int32),
            vmem((COARSE_SLOTS, 256), jnp.int32),
            vmem((256, 128), jnp.int32),
            pltpu.SMEM((RING, STEP, 128), jnp.int32),
            vmem((256, 256), F32),
            vmem((256, 256), F32),
            vmem((256, 128), F32),
            vmem((TARGETS // 8, 256), F32),
            vmem((256, 256), F32),
            vmem((128, 256), jnp.int32),
            vmem((3, TARGETS * NOPS, 256), BF16),
            vmem((NOPS, TARGETS, COEFFS), F32),
            vmem((STEP * 64, 128), F32),
            vmem((STEP * 64, 128), F32),
            vmem((NOPS, TARGETS, COEFFS), BF16),
            pltpu.SemaphoreType.DMA((9,)),
            pltpu.SemaphoreType.DMA((RING,)),
            pltpu.SemaphoreType.DMA((2, 3, 3)),
            pltpu.SemaphoreType.DMA((2, 3, 3)),
            pltpu.SemaphoreType.DMA((2, 4)),
            pltpu.SemaphoreType.DMA((2, 4)),
            pltpu.SemaphoreType.DMA((2,)),
            pltpu.SemaphoreType.DMA((2,)),
        ],
        compiler_params=pltpu.CompilerParams(
            collective_id=0, has_side_effects=True, vmem_limit_bytes=60 * 1024 * 1024
        ),
        cost_estimate=pl.CostEstimate(flops=14_000_000_000, bytes_accessed=12_000_000, transcendentals=0),
    )(
        multipole, coarse_multipole, operators, source_list.T, op_list.T, list_count.reshape(1, TARGETS),
        coarse_src.T, coarse_op.T,
    )


def solution(mesh):
    blocks = P(("gx", "gy"), None)
    placed = (blocks, blocks, P(), blocks, blocks, P(("gx", "gy")), blocks, blocks)
    return jax.shard_map(local, mesh=mesh, in_specs=placed, out_specs=blocks, check_vma=False)
```
